32 devices in a mesh: seq: 8 (over z, y), head: 4 (over x, core).
Axes of the slice: x: 2, y: 2, z: 4, core: 2. Of those that a mesh axis runs over, the one named last changes fastest.
Arguments:
- queries: bfloat16 [4096, 2048], P('seq', 'head'), may hold values from -6 to 6
- key_pairs: bfloat16 [4096, 2, 2048], P('seq', None, 'head'), may hold values from -6 to 6
- value_pairs: bfloat16 [4096, 2, 2048], P('seq', None, 'head'), may hold values from -0.375 to 0.375
- init_state: float32 [16, 128, 128], P('head'), may hold values from -6 to 6
- out_weight: bfloat16 [2048, 2048], replicated, may hold values from -0.125 to 0.125
Outputs:
- projected: bfloat16 [4096, 2048], P('seq', 'head')
The draws below stay inside these ranges and needn't reach their ends.
All inputs are finite; a program needn't handle non-finite values.
Results may differ from the reference program's by a relative error of at most 0.0085.
Values may be sent and summed in bfloat16 or wider, within the bound.
A program may use at most 128 MiB of HBM per device.

```python
import jax
import jax.numpy as jnp
from jax import lax

DMODEL = 2048
HEADS = 16
HEAD_DIM = 128
BLOCK = 32
TOKENS = 4096


def levels(stream_key, dims, cuts, least, high):
    gain, own = 1.0, jax.random.fold_in(stream_key, 6)
    for dim, shards_of in cuts:
        heights = jnp.exp(jax.random.uniform(jax.random.fold_in(own, dim), (shards_of,), jnp.float32, least / len(cuts), high / len(cuts)))
        gain = gain * jnp.repeat(heights, dims[dim] // shards_of).reshape([-1 if axis == dim else 1 for axis in range(len(dims))])
    return gain


def scatter_about(key, extent, width, most, cuts=(), kind=jnp.bfloat16):
    values = jax.random.normal(key, extent, jnp.float32) * width
    if len(cuts) > 0:
        values = levels(key, extent, cuts, -0.22, 0.18) * values
    return jnp.clip(values, min=-most, max=most).astype(kind)


def setup_inputs(seed: int = 0) -> dict:
    splits = jax.random.split(jax.random.key(seed), 6)
    return {
        "queries": scatter_about(splits[0], (TOKENS, HEADS * HEAD_DIM), 1.0, 6.0, ((0, 8), (1, 4))),
        "key_pairs": scatter_about(splits[1], (TOKENS, 2, HEADS * HEAD_DIM), 1.0, 6.0, ((0, 8), (2, 4))),
        "value_pairs": scatter_about(splits[2], (TOKENS, 2, HEADS * HEAD_DIM), ((8 * TOKENS // HEAD_DIM) ** -0.5), 0.375, ((0, 8), (2, 4))),
        "init_state": scatter_about(splits[3], (HEADS, HEAD_DIM, HEAD_DIM), 1.0, 6.0, ((0, 4),), jnp.float32),
        "out_weight": scatter_about(splits[4], (HEADS * HEAD_DIM, DMODEL), (HEADS * HEAD_DIM) ** -0.5, 0.125),
    }


epsilon = 1e-06

def product(left, right, pattern):
    return jnp.einsum(pattern, left, right, precision=lax.Precision.HIGHEST)

def unit_rows(entries):
    return entries * lax.rsqrt(lax.optimization_barrier(jnp.sum(entries * entries, axis=-1, keepdims=True)) + epsilon)

def block_parts(query_block, key_block, value_block):
    query_block = unit_rows(query_block.astype(jnp.float32))
    key_block = unit_rows(key_block.astype(jnp.float32))
    value_block = value_block.astype(jnp.float32)
    state_width = key_block.shape[-1]
    micro_len = key_block.shape[-2]
    gram = product(key_block, key_block, '...id,...jd->...ij')
    strict = jnp.tril(jnp.ones((micro_len, micro_len), jnp.float32), -1)
    system = jnp.eye(micro_len, dtype=jnp.float32) + 2.0 * gram * strict
    stacked = 2.0 * jnp.concatenate([key_block, value_block], axis=-1)
    system = jnp.broadcast_to(system, stacked.shape[:-1] + (micro_len,))
    solved = jax.scipy.linalg.solve_triangular(system, stacked, lower=True, unit_diagonal=True)
    writes = solved[..., :state_width]
    updates = solved[..., state_width:]
    scores = product(query_block, key_block, '...id,...jd->...ij')
    row_index = lax.broadcasted_iota(jnp.int32, (query_block.shape[-2], micro_len), 0)
    col_index = lax.broadcasted_iota(jnp.int32, (query_block.shape[-2], micro_len), 1)
    scores = jnp.where(col_index <= 2 * row_index + 1, scores, jnp.zeros_like(scores))
    adjusted = query_block - product(scores, writes, '...ij,...jd->...id')
    inside = product(scores, updates, '...ij,...jd->...id')
    moving = jnp.eye(state_width, dtype=jnp.float32) - product(key_block, writes, '...cd,...ce->...de')
    carried = product(key_block, updates, '...cd,...ce->...de')
    return (adjusted, inside, moving, carried)

def arrange(queries, key_pairs, value_pairs):
    tokens = queries.shape[0]
    head_count = queries.shape[1] // HEAD_DIM
    blocks = tokens // BLOCK
    query_blocks = jnp.transpose(queries.reshape(blocks, BLOCK, head_count, HEAD_DIM), (2, 0, 1, 3))
    key_blocks = jnp.transpose(key_pairs.reshape(blocks, 2 * BLOCK, head_count, HEAD_DIM), (2, 0, 1, 3))
    value_blocks = jnp.transpose(value_pairs.reshape(blocks, 2 * BLOCK, head_count, HEAD_DIM), (2, 0, 1, 3))
    return (query_blocks, key_blocks, value_blocks)

def reference(queries, key_pairs, value_pairs, init_state, out_weight):
    query_blocks, key_blocks, value_blocks = arrange(queries, key_pairs, value_pairs)

    def advance(state, inputs):
        adjusted, inside, moving, carried = block_parts(inputs[0], inputs[1], inputs[2])
        attended = product(adjusted, state, 'hcd,hde->hce') + inside
        following = product(moving, state, 'hij,hjk->hik') + carried
        return (following, attended)
    inputs = (jnp.moveaxis(query_blocks, 1, 0), jnp.moveaxis(key_blocks, 1, 0), jnp.moveaxis(value_blocks, 1, 0))
    final_state, outputs = lax.scan(advance, init_state.astype(jnp.float32), inputs)
    attended = jnp.transpose(outputs, (0, 2, 1, 3)).reshape(TOKENS, HEADS * HEAD_DIM).astype(jnp.bfloat16)
    return jnp.dot(attended.astype(jnp.float32), out_weight.astype(jnp.float32), preferred_element_type=jnp.float32).astype(jnp.bfloat16)
```

```python
import functools

import jax
import jax.numpy as jnp
from jax import lax
from jax.experimental import pallas as pl
from jax.experimental.pallas import tpu as pltpu
from jax.sharding import PartitionSpec as P

WIDTH = 128
CHUNK = 64
MICRO = 2 * CHUNK
SMALL = 8
epsilon = 1e-06
f32, bf16 = jnp.float32, jnp.bfloat16


def dot(a, b, dims=((1,), (0,))):
    return lax.dot_general(a, b, (dims, ((), ())), preferred_element_type=f32)


def split(x):
    high = x.astype(bf16)
    return high, (x - high.astype(f32)).astype(bf16)


def wide_left(x):
    return jnp.concatenate(split(x), axis=1)


def wide_right(y):
    row = jnp.concatenate(split(y), axis=1)
    return jnp.concatenate([row, row], axis=0)


def exact_product(x, y):
    both = dot(wide_left(x), wide_right(y))
    half = y.shape[1]
    return both[:, :half] + both[:, half:]


def iota(shape, dim):
    return lax.broadcasted_iota(jnp.int32, shape, dim)


def small_inverse(lower):
    row, col = iota((MICRO, WIDTH), 0), iota((MICRO, WIDTH), 1)
    same = row // SMALL == col // SMALL
    packed = jnp.where(same, lower, 0.0).reshape(MICRO // SMALL, SMALL, WIDTH).sum(0)
    sub, lane = iota((SMALL, WIDTH), 0), iota((SMALL, WIDTH), 1)
    inverse = jnp.where(lane % SMALL == sub, 1.0, 0.0).astype(f32)
    for c in range(SMALL - 1):
        factor = jnp.take_along_axis(packed, lane // SMALL * SMALL + c, axis=1, mode="promise_in_bounds")
        inverse = inverse - factor * inverse[c : c + 1]
    return jnp.where(same, jnp.concatenate([inverse] * (MICRO // SMALL), axis=0), 0.0)


def odd_rows(x, b):
    return jnp.concatenate([x[i : i + b] for i in range(b, MICRO, 2 * b)], axis=0)


def weave(even, odd, b):
    rows = []
    for i in range(0, MICRO // 2, b):
        rows += [even[i : i + b], odd[i : i + b]]
    return jnp.concatenate(rows, axis=0)


def even_rows(x, b):
    return jnp.concatenate([x[i : i + b] for i in range(0, MICRO, 2 * b)], axis=0)


def unit_lower_inverses(lowers):
    inverses = [small_inverse(lower) for lower in lowers]
    half = MICRO // 2
    row, col = iota((half, WIDTH), 0), iota((half, WIDTH), 1)
    zeros = jnp.zeros((half, WIDTH), f32)
    b = SMALL
    while b < MICRO:
        below = col // b == row // b * 2
        firsts = [
            exact_product(jnp.where(below, odd_rows(lower, b), 0.0), inverse)
            for lower, inverse in zip(lowers, inverses)
        ]
        odds = [odd_rows(inverse, b) for inverse in inverses]
        seconds = [
            odd - exact_product(odd, weave(zeros, first, b)) for odd, first in zip(odds, firsts)
        ]
        inverses = [
            weave(even_rows(inverse, b), second, b) for inverse, second in zip(inverses, seconds)
        ]
        b *= 2
    return inverses


def chunk_kernel(heads, per_step, q_ref, k_ref, v_ref, a_ref, o_ref, map_ref, z_ref):
    step = pl.program_id(0)
    row, col = iota((MICRO, WIDTH), 0), iota((MICRO, WIDTH), 1)
    eye = jnp.where(row == col, 1.0, 0.0).astype(f32)

    @pl.when(step == 0)
    def _():
        for h in range(heads):
            z_ref[h] = jnp.concatenate([eye, jnp.zeros((WIDTH, WIDTH), f32)], axis=1)

    where = [(p, h) for p in range(per_step) for h in range(heads)]

    def key_of(p, h):
        return k_ref[p * MICRO : (p + 1) * MICRO, h * WIDTH : (h + 1) * WIDTH]

    lowers, scales = [], []
    for p, h in where:
        key = key_of(p, h)
        gram = dot(key, key, ((1,), (1,)))
        diagonal = jnp.where(row == col, gram, 0.0)
        down = lax.rsqrt(jnp.sum(diagonal, axis=1, keepdims=True) + epsilon)
        across = lax.rsqrt(jnp.sum(diagonal, axis=0, keepdims=True) + epsilon)
        lowers.append(jnp.where(row > col, 2.0 * gram * down * across, 0.0))
        scales.append((down, across))
    inverses = unit_lower_inverses(lowers)
    prepared = []
    for (p, h), inverse, (down, across) in zip(where, inverses, scales):
        key = key_of(p, h)
        value = v_ref[p * MICRO : (p + 1) * MICRO, h * WIDTH : (h + 1) * WIDTH]
        inverse = inverse * (2.0 * down)
        write_key = dot(wide_left(inverse * across), jnp.concatenate([key, key], axis=0))
        write_value = dot(wide_left(inverse), jnp.concatenate([value, value], axis=0))
        (wk_high, wk_low), (wv_high, wv_low) = split(write_key), split(write_value)
        effect = dot(
            key, jnp.concatenate([wk_high, wv_high, wk_low, wv_low], axis=1), ((0,), (0,))
        )
        effect = effect[:, : 2 * WIDTH] + effect[:, 2 * WIDTH :]
        move, carry = eye - effect[:, :WIDTH], effect[:, WIDTH:]
        query = q_ref[p * CHUNK : (p + 1) * CHUNK, h * WIDTH : (h + 1) * WIDTH]
        scores = dot(query, key, ((1,), (1,)))
        token, micro = iota((CHUNK, MICRO), 0), iota((CHUNK, MICRO), 1)
        scores = jnp.where(micro <= 2 * token + 1, scores, 0.0).astype(bf16)
        inner = dot(scores, jnp.concatenate([wk_high, wv_high], axis=1))
        query = query.astype(f32)
        size = lax.rsqrt(jnp.sum(query * query, axis=1, keepdims=True) + epsilon)
        adjusted = (query - inner[:, :WIDTH]) * size
        prepared.append((wide_left(move), carry, adjusted.astype(bf16), inner[:, WIDTH:] * size))
    for (p, h), (move, carry, adjusted, inside) in zip(where, prepared):
        state = z_ref[h]
        high, low = split(state)
        out = dot(adjusted, high)
        here = (slice(p * CHUNK, (p + 1) * CHUNK), slice(h * WIDTH, (h + 1) * WIDTH))
        a_ref[here] = out[:, :WIDTH].astype(bf16)
        o_ref[here] = (out[:, WIDTH:] + inside).astype(o_ref.dtype)
        both = jnp.concatenate([high, low], axis=1)
        moved = dot(move, jnp.concatenate([both, both], axis=0))
        moved = moved[:, : 2 * WIDTH] + moved[:, 2 * WIDTH :]
        z_ref[h] = jnp.concatenate([moved[:, :WIDTH], moved[:, WIDTH:] + carry], axis=1)

    @pl.when(step == pl.num_programs(0) - 1)
    def _():
        map_ref[...] = z_ref[...].astype(map_ref.dtype)


def chunk_maps(queries, keys, values, wire):
    tokens, width = queries.shape
    heads = width // WIDTH
    per_step = 2
    rows = per_step * CHUNK
    return pl.pallas_call(
        functools.partial(chunk_kernel, heads, per_step),
        grid=(tokens // rows,),
        in_specs=[
            pl.BlockSpec((rows, width), lambda i: (i, 0)),
            pl.BlockSpec((2 * rows, width), lambda i: (i, 0)),
            pl.BlockSpec((2 * rows, width), lambda i: (i, 0)),
        ],
        out_specs=[
            pl.BlockSpec((rows, width), lambda i: (i, 0)),
            pl.BlockSpec((rows, width), lambda i: (i, 0)),
            pl.BlockSpec((heads, WIDTH, 2 * WIDTH), lambda i: (0, 0, 0)),
        ],
        out_shape=[
            jax.ShapeDtypeStruct((tokens, width), bf16),
            jax.ShapeDtypeStruct((tokens, width), f32),
            jax.ShapeDtypeStruct((heads, WIDTH, 2 * WIDTH), wire),
        ],
        scratch_shapes=[pltpu.VMEM((heads, WIDTH, 2 * WIDTH), f32)],
        compiler_params=pltpu.CompilerParams(vmem_limit_bytes=40 * 2**20),
        name="chunk_maps",
    )(queries, keys, values)


def enter_kernel(heads, place_ref, maps_ref, init_ref, a_ref, o_ref, out_ref, s_ref):
    s_ref[...] = init_ref[...]

    def one(j, _):
        for h in range(heads):
            parts = maps_ref[j, h]
            state = jnp.concatenate(split(s_ref[h]), axis=1)
            if parts.dtype == bf16:
                moved = dot(parts[:, :WIDTH], state)
            else:
                moved = dot(wide_left(parts[:, :WIDTH]), jnp.concatenate([state, state], axis=0))
            s_ref[h] = moved[:, :WIDTH] + moved[:, WIDTH:] + parts[:, WIDTH:].astype(f32)
        return 0

    lax.fori_loop(0, place_ref[0], one, 0)
    for h in range(heads):
        cols = slice(h * WIDTH, (h + 1) * WIDTH)
        out_ref[:, cols] = (dot(a_ref[:, cols], s_ref[h].astype(bf16)) + o_ref[:, cols]).astype(bf16)


def enter(maps, init_state, a, o):
    heads = init_state.shape[0]
    vmem = pl.BlockSpec(memory_space=pltpu.VMEM)
    return pl.pallas_call(
        functools.partial(enter_kernel, heads),
        in_specs=[pl.BlockSpec(memory_space=pltpu.SMEM)] + [vmem] * 4,
        out_specs=vmem,
        out_shape=jax.ShapeDtypeStruct(a.shape, bf16),
        scratch_shapes=[pltpu.VMEM(init_state.shape, f32)],
        compiler_params=pltpu.CompilerParams(vmem_limit_bytes=40 * 2**20),
        name="enter",
    )(lax.axis_index("seq").reshape(1).astype(jnp.int32), maps, init_state, a, o)


def local(queries, key_pairs, value_pairs, init_state, out_weight):
    tokens, width = queries.shape
    wire = bf16 if lax.axis_size("seq") <= 8 else f32
    keys = key_pairs.reshape(2 * tokens, width)
    values = value_pairs.reshape(2 * tokens, width)
    a, o, maps = chunk_maps(queries, keys, values, wire)
    attended = enter(lax.all_gather(maps, "seq"), init_state, a, o)
    model_cols = out_weight.shape[1] // lax.axis_size("head")
    own_cols = lax.dynamic_slice_in_dim(
        out_weight, lax.axis_index("head") * model_cols, model_cols, 1
    )
    return jnp.dot(
        lax.all_gather(attended, "head", axis=1, tiled=True),
        own_cols,
        preferred_element_type=jnp.float32,
    ).astype(jnp.bfloat16)


def solution(mesh):
    in_specs = (
        P("seq", "head"),
        P("seq", None, "head"),
        P("seq", None, "head"),
        P("head", None, None),
        P(),
    )
    out_specs = P("seq", "head")
    return jax.shard_map(local, mesh=mesh, in_specs=in_specs, out_specs=out_specs, check_vma=False)
```

```python
import functools

import jax
import jax.numpy as jnp
from jax import lax
from jax.experimental import pallas as pl
from jax.experimental.pallas import tpu as pltpu
from jax.sharding import PartitionSpec as P

WIDTH = 128
CHUNK = 64
MICRO = 2 * CHUNK
SMALL = 8
epsilon = 1e-06
f32, bf16 = jnp.float32, jnp.bfloat16


def dot(a, b, dims=((1,), (0,))):
    return lax.dot_general(a, b, (dims, ((), ())), preferred_element_type=f32)


def split(x):
    high = x.astype(bf16)
    return high, (x - high.astype(f32)).astype(bf16)


def wide_left(x):
    return jnp.concatenate(split(x), axis=1)


def wide_right(y):
    row = jnp.concatenate(split(y), axis=1)
    return jnp.concatenate([row, row], axis=0)


def exact_product(x, y):
    both = dot(wide_left(x), wide_right(y))
    half = y.shape[1]
    return both[:, :half] + both[:, half:]


def iota(shape, dim):
    return lax.broadcasted_iota(jnp.int32, shape, dim)


def small_inverse(lower):
    row, col = iota((MICRO, WIDTH), 0), iota((MICRO, WIDTH), 1)
    same = row // SMALL == col // SMALL
    packed = jnp.where(same, lower, 0.0).reshape(MICRO // SMALL, SMALL, WIDTH).sum(0)
    sub, lane = iota((SMALL, WIDTH), 0), iota((SMALL, WIDTH), 1)
    inverse = jnp.where(lane % SMALL == sub, 1.0, 0.0).astype(f32)
    for c in range(SMALL - 1):
        factor = jnp.take_along_axis(packed, lane // SMALL * SMALL + c, axis=1, mode="promise_in_bounds")
        inverse = inverse - factor * inverse[c : c + 1]
    return jnp.where(same, jnp.concatenate([inverse] * (MICRO // SMALL), axis=0), 0.0)


def odd_rows(x, b):
    return jnp.concatenate([x[i : i + b] for i in range(b, MICRO, 2 * b)], axis=0)


def weave(even, odd, b):
    rows = []
    for i in range(0, MICRO // 2, b):
        rows += [even[i : i + b], odd[i : i + b]]
    return jnp.concatenate(rows, axis=0)


def even_rows(x, b):
    return jnp.concatenate([x[i : i + b] for i in range(0, MICRO, 2 * b)], axis=0)


def unit_lower_inverses(lowers):
    inverses = [small_inverse(lower) for lower in lowers]
    half = MICRO // 2
    row, col = iota((half, WIDTH), 0), iota((half, WIDTH), 1)
    zeros = jnp.zeros((half, WIDTH), f32)
    b = SMALL
    while b < MICRO:
        below = col // b == row // b * 2
        firsts = [
            exact_product(jnp.where(below, odd_rows(lower, b), 0.0), inverse)
            for lower, inverse in zip(lowers, inverses)
        ]
        odds = [odd_rows(inverse, b) for inverse in inverses]
        seconds = [
            odd - exact_product(odd, weave(zeros, first, b)) for odd, first in zip(odds, firsts)
        ]
        inverses = [
            weave(even_rows(inverse, b), second, b) for inverse, second in zip(inverses, seconds)
        ]
        b *= 2
    return inverses


def chunk_kernel(heads, per_step, q_ref, k_ref, v_ref, a_ref, o_ref, map_ref, z_ref):
    step = pl.program_id(0)
    row, col = iota((MICRO, WIDTH), 0), iota((MICRO, WIDTH), 1)
    eye = jnp.where(row == col, 1.0, 0.0).astype(f32)

    @pl.when(step == 0)
    def _():
        for h in range(heads):
            z_ref[h] = jnp.concatenate([eye, jnp.zeros((WIDTH, WIDTH), f32)], axis=1)

    where = [(p, h) for p in range(per_step) for h in range(heads)]

    def key_of(p, h):
        return k_ref[p * MICRO : (p + 1) * MICRO, h * WIDTH : (h + 1) * WIDTH]

    lowers, scales = [], []
    for p, h in where:
        key = key_of(p, h)
        gram = dot(key, key, ((1,), (1,)))
        diagonal = jnp.where(row == col, gram, 0.0)
        down = lax.rsqrt(jnp.sum(diagonal, axis=1, keepdims=True) + epsilon)
        across = lax.rsqrt(jnp.sum(diagonal, axis=0, keepdims=True) + epsilon)
        lowers.append(jnp.where(row > col, 2.0 * gram * down * across, 0.0))
        scales.append((down, across))
    inverses = unit_lower_inverses(lowers)
    prepared = []
    for (p, h), inverse, (down, across) in zip(where, inverses, scales):
        key = key_of(p, h)
        value = v_ref[p * MICRO : (p + 1) * MICRO, h * WIDTH : (h + 1) * WIDTH]
        inverse = inverse * (2.0 * down)
        write_key = dot(wide_left(inverse * across), jnp.concatenate([key, key], axis=0))
        write_value = dot(wide_left(inverse), jnp.concatenate([value, value], axis=0))
        (wk_high, wk_low), (wv_high, wv_low) = split(write_key), split(write_value)
        effect = dot(
            key, jnp.concatenate([wk_high, wv_high, wk_low, wv_low], axis=1), ((0,), (0,))
        )
        effect = effect[:, : 2 * WIDTH] + effect[:, 2 * WIDTH :]
        move, carry = eye - effect[:, :WIDTH], effect[:, WIDTH:]
        query = q_ref[p * CHUNK : (p + 1) * CHUNK, h * WIDTH : (h + 1) * WIDTH]
        scores = dot(query, key, ((1,), (1,)))
        token, micro = iota((CHUNK, MICRO), 0), iota((CHUNK, MICRO), 1)
        scores = jnp.where(micro <= 2 * token + 1, scores, 0.0).astype(bf16)
        inner = dot(scores, jnp.concatenate([wk_high, wv_high], axis=1))
        query = query.astype(f32)
        size = lax.rsqrt(jnp.sum(query * query, axis=1, keepdims=True) + epsilon)
        adjusted = (query - inner[:, :WIDTH]) * size
        prepared.append((wide_left(move), carry, adjusted.astype(bf16), inner[:, WIDTH:] * size))
    for (p, h), (move, carry, adjusted, inside) in zip(where, prepared):
        state = z_ref[h]
        high, low = split(state)
        out = dot(adjusted, high)
        here = (slice(p * CHUNK, (p + 1) * CHUNK), slice(h * WIDTH, (h + 1) * WIDTH))
        a_ref[here] = out[:, :WIDTH].astype(bf16)
        o_ref[here] = (out[:, WIDTH:] + inside).astype(o_ref.dtype)
        both = jnp.concatenate([high, low], axis=1)
        moved = dot(move, jnp.concatenate([both, both], axis=0))
        moved = moved[:, : 2 * WIDTH] + moved[:, 2 * WIDTH :]
        z_ref[h] = jnp.concatenate([moved[:, :WIDTH], moved[:, WIDTH:] + carry], axis=1)

    @pl.when(step == pl.num_programs(0) - 1)
    def _():
        map_ref[...] = z_ref[...].astype(map_ref.dtype)


def chunk_maps(queries, keys, values, wire):
    tokens, width = queries.shape
    heads = width // WIDTH
    per_step = 2
    rows = per_step * CHUNK
    return pl.pallas_call(
        functools.partial(chunk_kernel, heads, per_step),
        grid=(tokens // rows,),
        in_specs=[
            pl.BlockSpec((rows, width), lambda i: (i, 0)),
            pl.BlockSpec((2 * rows, width), lambda i: (i, 0)),
            pl.BlockSpec((2 * rows, width), lambda i: (i, 0)),
        ],
        out_specs=[
            pl.BlockSpec((rows, width), lambda i: (i, 0)),
            pl.BlockSpec((rows, width), lambda i: (i, 0)),
            pl.BlockSpec((heads, WIDTH, 2 * WIDTH), lambda i: (0, 0, 0)),
        ],
        out_shape=[
            jax.ShapeDtypeStruct((tokens, width), bf16),
            jax.ShapeDtypeStruct((tokens, width), f32),
            jax.ShapeDtypeStruct((heads, WIDTH, 2 * WIDTH), wire),
        ],
        scratch_shapes=[pltpu.VMEM((heads, WIDTH, 2 * WIDTH), f32)],
        compiler_params=pltpu.CompilerParams(vmem_limit_bytes=40 * 2**20),
        name="chunk_maps",
    )(queries, keys, values)


def finish_kernel(
    shards, heads, maps_ref, init_ref, a_ref, o_ref, w_hbm, out_ref,
    w_ref, move_ref, state_ref, wire_out, wire_in, att_ref, acc_ref,
    w_sem, chain_send, chain_recv, att_send, att_recv,
):
    place, group = lax.axis_index("seq"), lax.axis_index("head")
    across = lax.rem(group + 2, 4)
    beside = group + 1 - 2 * lax.rem(group, 2)
    beyond = lax.rem(beside + 2, 4)
    depth, cols = heads * WIDTH, out_ref.shape[1]
    w_copy = pltpu.make_async_copy(
        w_hbm.at[:, pl.ds(pl.multiple_of(group * cols, cols), cols)], w_ref, w_sem
    )
    w_copy.start()

    barrier = pltpu.get_barrier_semaphore()

    def greet(target):
        pl.semaphore_signal(barrier, inc=1, device_id=target, device_id_type=pl.DeviceIdType.MESH)

    greet((place, across))
    greet((place, beside))

    @pl.when(place > 0)
    def _():
        greet((place - 1, group))

    @pl.when(place < shards - 1)
    def _():
        greet((place + 1, group))

    for h in range(heads):
        move_ref[h] = wide_left(maps_ref[h, :, :WIDTH])

    ends = jnp.where(place == 0, 1, 0) + jnp.where(place == shards - 1, 1, 0)
    pl.semaphore_wait(barrier, 4 - ends)

    def chain(h):
        return pltpu.make_async_remote_copy(
            src_ref=wire_out.at[h], dst_ref=wire_in.at[h],
            send_sem=chain_send.at[h], recv_sem=chain_recv.at[h],
            device_id=(place + 1, group), device_id_type=pl.DeviceIdType.MESH,
        )

    def pass_on(source, slot, h, target):
        return pltpu.make_async_remote_copy(
            src_ref=att_ref.at[source, h], dst_ref=att_ref.at[slot, h],
            send_sem=att_send.at[slot, h], recv_sem=att_recv.at[slot, h],
            device_id=(place, target), device_id_type=pl.DeviceIdType.MESH,
        )

    to_across = [pass_on(0, 1, h, across) for h in range(heads)]
    to_beside = [pass_on(0, 2, h, beside) for h in range(heads)]
    relayed = [pass_on(1, 3, h, beside) for h in range(heads)]

    for h in range(heads):

        @pl.when(place == 0)
        def _():
            state_ref[h] = init_ref[h]

        @pl.when(place > 0)
        def _():
            chain(h).wait_recv()
            state_ref[h] = wire_in[h].astype(f32)

        @pl.when(place < shards - 1)
        def _():
            both = jnp.concatenate(split(state_ref[h]), axis=1)
            moved = dot(move_ref[h], jnp.concatenate([both, both], axis=0))
            moved = moved[:, :WIDTH] + moved[:, WIDTH:] + maps_ref[h, :, WIDTH:]
            wire_out[h] = moved.astype(wire_out.dtype)
            chain(h).start()

        here = slice(h * WIDTH, (h + 1) * WIDTH)
        att_ref[0, h] = (
            dot(a_ref[:, here], state_ref[h].astype(bf16)) + o_ref[:, here]
        ).astype(bf16)
        to_across[h].start()
        to_beside[h].start()

    w_copy.wait()

    def project(slot, owner, first, count):
        rows = pl.multiple_of(owner * depth, depth) + first * WIDTH
        left = jnp.concatenate([att_ref[slot, first + i] for i in range(count)], axis=1)
        return dot(left, w_ref[pl.ds(pl.multiple_of(rows, WIDTH), count * WIDTH), :])

    acc_ref[...] = project(0, group, 0, heads)
    for h in range(heads):
        to_across[h].wait_recv()
        relayed[h].start()
        if h == 0:
            for i in range(heads):
                to_beside[i].wait_recv()
            acc_ref[...] += project(2, beside, 0, heads)
        if h % 2 == 1:
            acc_ref[...] += project(1, across, h - 1, 2)
            if h > 1:
                relayed[h - 3].wait_recv()
                relayed[h - 2].wait_recv()
                acc_ref[...] += project(3, beyond, h - 3, 2)
    relayed[heads - 2].wait_recv()
    relayed[heads - 1].wait_recv()
    out_ref[...] = (acc_ref[...] + project(3, beyond, heads - 2, 2)).astype(bf16)
    for h in range(heads):
        to_across[h].wait_send()
        to_beside[h].wait_send()
        relayed[h].wait_send()

        @pl.when(place < shards - 1)
        def _():
            chain(h).wait_send()


def finish(maps, init_state, a, o, out_weight, wire):
    heads = init_state.shape[0]
    shards = lax.axis_size("seq")
    tokens = a.shape[0]
    features = out_weight.shape[0]
    cols = out_weight.shape[1] // lax.axis_size("head")
    vmem = pl.BlockSpec(memory_space=pltpu.VMEM)
    dma = pltpu.SemaphoreType.DMA
    return pl.pallas_call(
        functools.partial(finish_kernel, shards, heads),
        in_specs=[vmem] * 4 + [pl.BlockSpec(memory_space=pl.ANY)],
        out_specs=vmem,
        out_shape=jax.ShapeDtypeStruct((tokens, cols), bf16),
        scratch_shapes=[
            pltpu.VMEM((features, cols), bf16),
            pltpu.VMEM((heads, WIDTH, 2 * WIDTH), bf16),
            pltpu.VMEM((heads, WIDTH, WIDTH), f32),
            pltpu.VMEM((heads, WIDTH, WIDTH), wire),
            pltpu.VMEM((heads, WIDTH, WIDTH), wire),
            pltpu.VMEM((4, heads, tokens, WIDTH), bf16),
            pltpu.VMEM((tokens, cols), f32),
            dma, dma((heads,)), dma((heads,)), dma((4, heads)), dma((4, heads)),
        ],
        compiler_params=pltpu.CompilerParams(
            vmem_limit_bytes=40 * 2**20, collective_id=0, has_side_effects=True
        ),
        name="finish",
    )(maps, init_state, a, o, out_weight)


def local(queries, key_pairs, value_pairs, init_state, out_weight):
    tokens, width = queries.shape
    wire = bf16 if lax.axis_size("seq") <= 8 else f32
    keys = key_pairs.reshape(2 * tokens, width)
    values = value_pairs.reshape(2 * tokens, width)
    a, o, maps = chunk_maps(queries, keys, values, f32)
    return finish(maps, init_state, a, o, out_weight, wire)


def solution(mesh):
    in_specs = (
        P("seq", "head"),
        P("seq", None, "head"),
        P("seq", None, "head"),
        P("head", None, None),
        P(),
    )
    out_specs = P("seq", "head")
    return jax.shard_map(local, mesh=mesh, in_specs=in_specs, out_specs=out_specs, check_vma=False)
```

```python
import functools

import jax
import jax.numpy as jnp
from jax import lax
from jax.experimental import pallas as pl
from jax.experimental.pallas import tpu as pltpu
from jax.sharding import PartitionSpec as P

WIDTH = 128
CHUNK = 64
MICRO = 2 * CHUNK
SMALL = 8
epsilon = 1e-06
f32, bf16 = jnp.float32, jnp.bfloat16


def dot(a, b, dims=((1,), (0,))):
    return lax.dot_general(a, b, (dims, ((), ())), preferred_element_type=f32)


def split(x):
    high = x.astype(bf16)
    return high, (x - high.astype(f32)).astype(bf16)


def wide_left(x):
    return jnp.concatenate(split(x), axis=1)


def wide_right(y):
    row = jnp.concatenate(split(y), axis=1)
    return jnp.concatenate([row, row], axis=0)


def exact_product(x, y):
    both = dot(wide_left(x), wide_right(y))
    half = y.shape[1]
    return both[:, :half] + both[:, half:]


def iota(shape, dim):
    return lax.broadcasted_iota(jnp.int32, shape, dim)


def small_inverse(lower):
    row, col = iota((MICRO, WIDTH), 0), iota((MICRO, WIDTH), 1)
    same = row // SMALL == col // SMALL
    packed = jnp.where(same, lower, 0.0).reshape(MICRO // SMALL, SMALL, WIDTH).sum(0)
    sub, lane = iota((SMALL, WIDTH), 0), iota((SMALL, WIDTH), 1)
    inverse = jnp.where(lane % SMALL == sub, 1.0, 0.0).astype(f32)
    for c in range(SMALL - 1):
        factor = jnp.take_along_axis(packed, lane // SMALL * SMALL + c, axis=1, mode="promise_in_bounds")
        inverse = inverse - factor * inverse[c : c + 1]
    return jnp.where(same, jnp.concatenate([inverse] * (MICRO // SMALL), axis=0), 0.0)


def odd_rows(x, b):
    return jnp.concatenate([x[i : i + b] for i in range(b, MICRO, 2 * b)], axis=0)


def weave(even, odd, b):
    rows = []
    for i in range(0, MICRO // 2, b):
        rows += [even[i : i + b], odd[i : i + b]]
    return jnp.concatenate(rows, axis=0)


def even_rows(x, b):
    return jnp.concatenate([x[i : i + b] for i in range(0, MICRO, 2 * b)], axis=0)


def unit_lower_inverses(lowers):
    inverses = [small_inverse(lower) for lower in lowers]
    half = MICRO // 2
    row, col = iota((half, WIDTH), 0), iota((half, WIDTH), 1)
    zeros = jnp.zeros((half, WIDTH), f32)
    b = SMALL
    while b < MICRO:
        below = col // b == row // b * 2
        firsts = [
            exact_product(jnp.where(below, odd_rows(lower, b), 0.0), inverse)
            for lower, inverse in zip(lowers, inverses)
        ]
        odds = [odd_rows(inverse, b) for inverse in inverses]
        seconds = [
            odd - exact_product(odd, weave(zeros, first, b)) for odd, first in zip(odds, firsts)
        ]
        inverses = [
            weave(even_rows(inverse, b), second, b) for inverse, second in zip(inverses, seconds)
        ]
        b *= 2
    return inverses


def pair_rows(ref, p, h):
    pairs = ref[p * CHUNK : (p + 1) * CHUNK, :, h * WIDTH : (h + 1) * WIDTH]
    return pairs.reshape(MICRO, WIDTH)


def chunk_kernel(heads, per_step, q_ref, k_ref, v_ref, a_ref, o_ref, map_ref, z_ref):
    step = pl.program_id(0)
    row, col = iota((MICRO, WIDTH), 0), iota((MICRO, WIDTH), 1)
    eye = jnp.where(row == col, 1.0, 0.0).astype(f32)

    @pl.when(step == 0)
    def _():
        for h in range(heads):
            z_ref[h] = jnp.concatenate([eye, jnp.zeros((WIDTH, WIDTH), f32)], axis=1)

    where = [(p, h) for p in range(per_step) for h in range(heads)]

    def key_of(p, h):
        return pair_rows(k_ref, p, h)

    lowers, scales = [], []
    for p, h in where:
        key = key_of(p, h)
        gram = dot(key, key, ((1,), (1,)))
        diagonal = jnp.where(row == col, gram, 0.0)
        down = lax.rsqrt(jnp.sum(diagonal, axis=1, keepdims=True) + epsilon)
        across = lax.rsqrt(jnp.sum(diagonal, axis=0, keepdims=True) + epsilon)
        lowers.append(jnp.where(row > col, 2.0 * gram * down * across, 0.0))
        scales.append((down, across))
    inverses = unit_lower_inverses(lowers)
    prepared = []
    for (p, h), inverse, (down, across) in zip(where, inverses, scales):
        key = key_of(p, h)
        value = pair_rows(v_ref, p, h)
        inverse = inverse * (2.0 * down)
        write_key = dot(wide_left(inverse * across), jnp.concatenate([key, key], axis=0))
        write_value = dot(wide_left(inverse), jnp.concatenate([value, value], axis=0))
        (wk_high, wk_low), (wv_high, wv_low) = split(write_key), split(write_value)
        effect = dot(
            key, jnp.concatenate([wk_high, wv_high, wk_low, wv_low], axis=1), ((0,), (0,))
        )
        effect = effect[:, : 2 * WIDTH] + effect[:, 2 * WIDTH :]
        move, carry = eye - effect[:, :WIDTH], effect[:, WIDTH:]
        query = q_ref[p * CHUNK : (p + 1) * CHUNK, h * WIDTH : (h + 1) * WIDTH]
        scores = dot(query, key, ((1,), (1,)))
        token, micro = iota((CHUNK, MICRO), 0), iota((CHUNK, MICRO), 1)
        scores = jnp.where(micro <= 2 * token + 1, scores, 0.0).astype(bf16)
        inner = dot(scores, jnp.concatenate([wk_high, wv_high], axis=1))
        query = query.astype(f32)
        size = lax.rsqrt(jnp.sum(query * query, axis=1, keepdims=True) + epsilon)
        adjusted = (query - inner[:, :WIDTH]) * size
        prepared.append((wide_left(move), carry, adjusted.astype(bf16), inner[:, WIDTH:] * size))
    for (p, h), (move, carry, adjusted, inside) in zip(where, prepared):
        state = z_ref[h]
        high, low = split(state)
        out = dot(adjusted, high)
        here = (slice(p * CHUNK, (p + 1) * CHUNK), slice(h * WIDTH, (h + 1) * WIDTH))
        a_ref[here] = out[:, :WIDTH].astype(bf16)
        o_ref[here] = (out[:, WIDTH:] + inside).astype(o_ref.dtype)
        both = jnp.concatenate([high, low], axis=1)
        moved = dot(move, jnp.concatenate([both, both], axis=0))
        moved = moved[:, : 2 * WIDTH] + moved[:, 2 * WIDTH :]
        z_ref[h] = jnp.concatenate([moved[:, :WIDTH], moved[:, WIDTH:] + carry], axis=1)

    @pl.when(step == pl.num_programs(0) - 1)
    def _():
        map_ref[...] = z_ref[...].astype(map_ref.dtype)


def chunk_maps(queries, keys, values, wire):
    tokens, width = queries.shape
    heads = width // WIDTH
    per_step = 2
    rows = per_step * CHUNK
    return pl.pallas_call(
        functools.partial(chunk_kernel, heads, per_step),
        grid=(tokens // rows,),
        in_specs=[
            pl.BlockSpec((rows, width), lambda i: (i, 0)),
            pl.BlockSpec((rows, 2, width), lambda i: (i, 0, 0)),
            pl.BlockSpec((rows, 2, width), lambda i: (i, 0, 0)),
        ],
        out_specs=[
            pl.BlockSpec((rows, width), lambda i: (i, 0)),
            pl.BlockSpec((rows, width), lambda i: (i, 0)),
            pl.BlockSpec((heads, WIDTH, 2 * WIDTH), lambda i: (0, 0, 0)),
        ],
        out_shape=[
            jax.ShapeDtypeStruct((tokens, width), bf16),
            jax.ShapeDtypeStruct((tokens, width), f32),
            jax.ShapeDtypeStruct((heads, WIDTH, 2 * WIDTH), wire),
        ],
        scratch_shapes=[pltpu.VMEM((heads, WIDTH, 2 * WIDTH), f32)],
        compiler_params=pltpu.CompilerParams(vmem_limit_bytes=56 * 2**20),
        name="chunk_maps",
    )(queries, keys, values)


def finish_kernel(
    shards, heads, maps_ref, init_ref, a_ref, o_ref, w_hbm, out_ref,
    w_ref, move_ref, state_ref, wire_out, wire_in, att_ref, acc_ref,
    w_sem, chain_send, chain_recv, att_send, att_recv,
):
    place, group = lax.axis_index("seq"), lax.axis_index("head")
    across = lax.rem(group + 2, 4)
    beside = group + 1 - 2 * lax.rem(group, 2)
    beyond = lax.rem(beside + 2, 4)
    depth, cols = heads * WIDTH, out_ref.shape[1]
    w_copy = pltpu.make_async_copy(
        w_hbm.at[:, pl.ds(pl.multiple_of(group * cols, cols), cols)], w_ref, w_sem
    )
    w_copy.start()

    barrier = pltpu.get_barrier_semaphore()

    def greet(target):
        pl.semaphore_signal(barrier, inc=1, device_id=target, device_id_type=pl.DeviceIdType.MESH)

    greet((place, across))
    greet((place, beside))

    @pl.when(place > 0)
    def _():
        greet((place - 1, group))

    @pl.when(place < shards - 1)
    def _():
        greet((place + 1, group))

    for h in range(heads):
        move_ref[h] = wide_left(maps_ref[h, :, :WIDTH])

    ends = jnp.where(place == 0, 1, 0) + jnp.where(place == shards - 1, 1, 0)
    pl.semaphore_wait(barrier, 4 - ends)

    def chain(h):
        return pltpu.make_async_remote_copy(
            src_ref=wire_out.at[h], dst_ref=wire_in.at[h],
            send_sem=chain_send.at[h], recv_sem=chain_recv.at[h],
            device_id=(place + 1, group), device_id_type=pl.DeviceIdType.MESH,
        )

    def pass_on(source, slot, h, target):
        return pltpu.make_async_remote_copy(
            src_ref=att_ref.at[source, h], dst_ref=att_ref.at[slot, h],
            send_sem=att_send.at[slot, h], recv_sem=att_recv.at[slot, h],
            device_id=(place, target), device_id_type=pl.DeviceIdType.MESH,
        )

    to_across = [pass_on(0, 1, h, across) for h in range(heads)]
    to_beside = [pass_on(0, 2, h, beside) for h in range(heads)]
    relayed = [pass_on(1, 3, h, beside) for h in range(heads)]

    for h in range(heads):

        @pl.when(place == 0)
        def _():
            state_ref[h] = init_ref[h]

        @pl.when(place > 0)
        def _():
            chain(h).wait_recv()
            state_ref[h] = wire_in[h].astype(f32)

        @pl.when(place < shards - 1)
        def _():
            both = jnp.concatenate(split(state_ref[h]), axis=1)
            moved = dot(move_ref[h], jnp.concatenate([both, both], axis=0))
            moved = moved[:, :WIDTH] + moved[:, WIDTH:] + maps_ref[h, :, WIDTH:]
            wire_out[h] = moved.astype(wire_out.dtype)
            chain(h).start()

        here = slice(h * WIDTH, (h + 1) * WIDTH)
        att_ref[0, h] = (
            dot(a_ref[:, here], state_ref[h].astype(bf16)) + o_ref[:, here]
        ).astype(bf16)
        to_across[h].start()
        to_beside[h].start()

    w_copy.wait()

    def project(slot, owner, first, count):
        rows = pl.multiple_of(owner * depth, depth) + first * WIDTH
        left = jnp.concatenate([att_ref[slot, first + i] for i in range(count)], axis=1)
        return dot(left, w_ref[pl.ds(pl.multiple_of(rows, WIDTH), count * WIDTH), :])

    acc_ref[...] = project(0, group, 0, heads)
    for h in range(heads):
        to_across[h].wait_recv()
        relayed[h].start()
        if h == 0:
            for i in range(heads):
                to_beside[i].wait_recv()
            acc_ref[...] += project(2, beside, 0, heads)
        if h % 2 == 1:
            acc_ref[...] += project(1, across, h - 1, 2)
            if h > 1:
                relayed[h - 3].wait_recv()
                relayed[h - 2].wait_recv()
                acc_ref[...] += project(3, beyond, h - 3, 2)
    relayed[heads - 2].wait_recv()
    relayed[heads - 1].wait_recv()
    out_ref[...] = (acc_ref[...] + project(3, beyond, heads - 2, 2)).astype(bf16)
    for h in range(heads):
        to_across[h].wait_send()
        to_beside[h].wait_send()
        relayed[h].wait_send()

        @pl.when(place < shards - 1)
        def _():
            chain(h).wait_send()


def finish(maps, init_state, a, o, out_weight, wire):
    heads = init_state.shape[0]
    shards = lax.axis_size("seq")
    tokens = a.shape[0]
    features = out_weight.shape[0]
    cols = out_weight.shape[1] // lax.axis_size("head")
    vmem = pl.BlockSpec(memory_space=pltpu.VMEM)
    dma = pltpu.SemaphoreType.DMA
    return pl.pallas_call(
        functools.partial(finish_kernel, shards, heads),
        in_specs=[vmem] * 4 + [pl.BlockSpec(memory_space=pl.ANY)],
        out_specs=vmem,
        out_shape=jax.ShapeDtypeStruct((tokens, cols), bf16),
        scratch_shapes=[
            pltpu.VMEM((features, cols), bf16),
            pltpu.VMEM((heads, WIDTH, 2 * WIDTH), bf16),
            pltpu.VMEM((heads, WIDTH, WIDTH), f32),
            pltpu.VMEM((heads, WIDTH, WIDTH), wire),
            pltpu.VMEM((heads, WIDTH, WIDTH), wire),
            pltpu.VMEM((4, heads, tokens, WIDTH), bf16),
            pltpu.VMEM((tokens, cols), f32),
            dma, dma((heads,)), dma((heads,)), dma((4, heads)), dma((4, heads)),
        ],
        compiler_params=pltpu.CompilerParams(
            vmem_limit_bytes=56 * 2**20, collective_id=0, has_side_effects=True
        ),
        name="finish",
    )(maps, init_state, a, o, out_weight)


def local(queries, key_pairs, value_pairs, init_state, out_weight):
    wire = bf16 if lax.axis_size("seq") <= 8 else f32
    a, o, maps = chunk_maps(queries, key_pairs, value_pairs, f32)
    return finish(maps, init_state, a, o, out_weight, wire)


def solution(mesh):
    in_specs = (
        P("seq", "head"),
        P("seq", None, "head"),
        P("seq", None, "head"),
        P("head", None, None),
        P(),
    )
    out_specs = P("seq", "head")
    return jax.shard_map(local, mesh=mesh, in_specs=in_specs, out_specs=out_specs, check_vma=False)
```

```python
import functools

import jax
import jax.numpy as jnp
from jax import lax
from jax.experimental import pallas as pl
from jax.experimental.pallas import tpu as pltpu
from jax.sharding import PartitionSpec as P

WIDTH = 128
CHUNK = 64
MICRO = 2 * CHUNK
SMALL = 8
epsilon = 1e-06
f32, bf16 = jnp.float32, jnp.bfloat16


def dot(a, b, dims=((1,), (0,))):
    return lax.dot_general(a, b, (dims, ((), ())), preferred_element_type=f32)


def split(x):
    high = x.astype(bf16)
    return high, (x - high.astype(f32)).astype(bf16)


def wide_left(x):
    return jnp.concatenate(split(x), axis=1)


def wide_right(y):
    row = jnp.concatenate(split(y), axis=1)
    return jnp.concatenate([row, row], axis=0)


def exact_product(x, y):
    both = dot(wide_left(x), wide_right(y))
    half = y.shape[1]
    return both[:, :half] + both[:, half:]


def iota(shape, dim):
    return lax.broadcasted_iota(jnp.int32, shape, dim)


def small_inverse(lower):
    row, col = iota((MICRO, WIDTH), 0), iota((MICRO, WIDTH), 1)
    same = row // SMALL == col // SMALL
    packed = jnp.where(same, lower, 0.0).reshape(MICRO // SMALL, SMALL, WIDTH).sum(0)
    sub, lane = iota((SMALL, WIDTH), 0), iota((SMALL, WIDTH), 1)
    inverse = jnp.where(lane % SMALL == sub, 1.0, 0.0).astype(f32)
    for c in range(SMALL - 1):
        factor = jnp.take_along_axis(packed, lane // SMALL * SMALL + c, axis=1, mode="promise_in_bounds")
        inverse = inverse - factor * inverse[c : c + 1]
    return jnp.where(same, jnp.concatenate([inverse] * (MICRO // SMALL), axis=0), 0.0)


def odd_rows(x, b):
    return jnp.concatenate([x[i : i + b] for i in range(b, MICRO, 2 * b)], axis=0)


def weave(even, odd, b):
    rows = []
    for i in range(0, MICRO // 2, b):
        rows += [even[i : i + b], odd[i : i + b]]
    return jnp.concatenate(rows, axis=0)


def even_rows(x, b):
    return jnp.concatenate([x[i : i + b] for i in range(0, MICRO, 2 * b)], axis=0)


def unit_lower_inverses(lowers):
    inverses = [small_inverse(lower) for lower in lowers]
    half = MICRO // 2
    row, col = iota((half, WIDTH), 0), iota((half, WIDTH), 1)
    zeros = jnp.zeros((half, WIDTH), f32)
    b = SMALL
    while b < MICRO:
        below = col // b == row // b * 2
        firsts = [
            exact_product(jnp.where(below, odd_rows(lower, b), 0.0), inverse)
            for lower, inverse in zip(lowers, inverses)
        ]
        odds = [odd_rows(inverse, b) for inverse in inverses]
        seconds = [
            odd - exact_product(odd, weave(zeros, first, b)) for odd, first in zip(odds, firsts)
        ]
        inverses = [
            weave(even_rows(inverse, b), second, b) for inverse, second in zip(inverses, seconds)
        ]
        b *= 2
    return inverses


def pair_rows(ref, p, h):
    pairs = ref[pl.ds(p * CHUNK, CHUNK), :, h * WIDTH : (h + 1) * WIDTH]
    return pairs.reshape(MICRO, WIDTH)


def advance(step, heads, per_step, k_ref, v_ref, z_ref, start_ref, write_ref):
    base = step * per_step
    row, col = iota((MICRO, WIDTH), 0), iota((MICRO, WIDTH), 1)
    eye = jnp.where(row == col, 1.0, 0.0).astype(f32)

    where = [(p, h) for p in range(per_step) for h in range(heads)]

    def key_of(p, h):
        return pair_rows(k_ref, base + p, h)

    lowers, scales = [], []
    for p, h in where:
        key = key_of(p, h)
        gram = dot(key, key, ((1,), (1,)))
        diagonal = jnp.where(row == col, gram, 0.0)
        down = lax.rsqrt(jnp.sum(diagonal, axis=1, keepdims=True) + epsilon)
        across = lax.rsqrt(jnp.sum(diagonal, axis=0, keepdims=True) + epsilon)
        lowers.append(jnp.where(row > col, 2.0 * gram * down * across, 0.0))
        scales.append((down, across))
    inverses = unit_lower_inverses(lowers)
    prepared = []
    for (p, h), inverse, (down, across) in zip(where, inverses, scales):
        key = key_of(p, h)
        value = pair_rows(v_ref, base + p, h)
        inverse = inverse * (2.0 * down)
        write_key = dot(wide_left(inverse * across), jnp.concatenate([key, key], axis=0))
        write_value = dot(wide_left(inverse), jnp.concatenate([value, value], axis=0))
        (wk_high, wk_low), (wv_high, wv_low) = split(write_key), split(write_value)
        effect = dot(
            key, jnp.concatenate([wk_high, wv_high, wk_low, wv_low], axis=1), ((0,), (0,))
        )
        effect = effect[:, : 2 * WIDTH] + effect[:, 2 * WIDTH :]
        move, carry = eye - effect[:, :WIDTH], effect[:, WIDTH:]
        write_ref[base + p, h] = jnp.concatenate([wk_high, wv_high], axis=1)
        prepared.append((wide_left(move), carry))
    for (p, h), (move, carry) in zip(where, prepared):
        high, low = split(z_ref[h])
        start_ref[base + p, h] = high
        both = jnp.concatenate([high, low], axis=1)
        moved = dot(move, jnp.concatenate([both, both], axis=0))
        moved = moved[:, : 2 * WIDTH] + moved[:, 2 * WIDTH :]
        z_ref[h] = jnp.concatenate([moved[:, :WIDTH], moved[:, WIDTH:] + carry], axis=1)


def prepare(chunk, heads, q_ref, k_ref, start_ref, write_ref, a_ref, o_ref):
    rows = pl.ds(pl.multiple_of(chunk * CHUNK, CHUNK), CHUNK)
    token, micro = iota((CHUNK, MICRO), 0), iota((CHUNK, MICRO), 1)
    for h in range(heads):
        cols = slice(h * WIDTH, (h + 1) * WIDTH)
        query = q_ref[rows, cols]
        scores = dot(query, pair_rows(k_ref, chunk, h), ((1,), (1,)))
        scores = jnp.where(micro <= 2 * token + 1, scores, 0.0).astype(bf16)
        inner = dot(scores, write_ref[chunk, h])
        query = query.astype(f32)
        size = lax.rsqrt(jnp.sum(query * query, axis=1, keepdims=True) + epsilon)
        adjusted = (query - inner[:, :WIDTH]) * size
        out = dot(adjusted.astype(bf16), start_ref[chunk, h])
        a_ref[rows, cols] = out[:, :WIDTH].astype(bf16)
        o_ref[rows, cols] = out[:, WIDTH:] + inner[:, WIDTH:] * size


def layer_kernel(
    shards, heads, q_ref, k_ref, v_ref, init_ref, w_hbm, out_ref,
    maps_ref, start_ref, write_ref, a_ref, o_ref, w_ref, move_ref, state_ref, wire_out, wire_in, att_ref, acc_ref,
    w_sem, chain_send, chain_recv, att_send, att_recv,
):
    place, group = lax.axis_index("seq"), lax.axis_index("head")
    across = lax.rem(group + 2, 4)
    beside = group + 1 - 2 * lax.rem(group, 2)
    beyond = lax.rem(beside + 2, 4)
    depth, cols = heads * WIDTH, out_ref.shape[1]
    w_copy = pltpu.make_async_copy(
        w_hbm.at[:, pl.ds(pl.multiple_of(group * cols, cols), cols)], w_ref, w_sem
    )
    w_copy.start()

    barrier = pltpu.get_barrier_semaphore()

    def greet(target):
        pl.semaphore_signal(barrier, inc=1, device_id=target, device_id_type=pl.DeviceIdType.MESH)

    greet((place, across))
    greet((place, beside))

    @pl.when(place > 0)
    def _():
        greet((place - 1, group))

    @pl.when(place < shards - 1)
    def _():
        greet((place + 1, group))

    chunks, per_step = q_ref.shape[0] // CHUNK, 2
    eye = jnp.where(iota((WIDTH, WIDTH), 0) == iota((WIDTH, WIDTH), 1), 1.0, 0.0).astype(f32)
    for h in range(heads):
        maps_ref[h] = jnp.concatenate([eye, jnp.zeros((WIDTH, WIDTH), f32)], axis=1)

    def one_step(step, _):
        advance(step, heads, per_step, k_ref, v_ref, maps_ref, start_ref, write_ref)
        return 0

    def one_chunk(chunk, _):
        prepare(chunk, heads, q_ref, k_ref, start_ref, write_ref, a_ref, o_ref)
        return 0

    lax.fori_loop(0, chunks // per_step, one_step, 0)
    for h in range(heads):
        move_ref[h] = wide_left(maps_ref[h, :, :WIDTH])

    ends = jnp.where(place == 0, 1, 0) + jnp.where(place == shards - 1, 1, 0)
    pl.semaphore_wait(barrier, 4 - ends)

    def chain(h):
        return pltpu.make_async_remote_copy(
            src_ref=wire_out.at[h], dst_ref=wire_in.at[h],
            send_sem=chain_send.at[h], recv_sem=chain_recv.at[h],
            device_id=(place + 1, group), device_id_type=pl.DeviceIdType.MESH,
        )

    def pass_on(source, slot, h, target):
        return pltpu.make_async_remote_copy(
            src_ref=att_ref.at[source, h], dst_ref=att_ref.at[slot, h],
            send_sem=att_send.at[slot, h], recv_sem=att_recv.at[slot, h],
            device_id=(place, target), device_id_type=pl.DeviceIdType.MESH,
        )

    to_across = [pass_on(0, 1, h, across) for h in range(heads)]
    to_beside = [pass_on(0, 2, h, beside) for h in range(heads)]
    relayed = [pass_on(1, 3, h, beside) for h in range(heads)]

    def attend(h):
        here = slice(h * WIDTH, (h + 1) * WIDTH)
        att_ref[0, h] = (
            dot(a_ref[:, here], state_ref[h].astype(bf16)) + o_ref[:, here]
        ).astype(bf16)
        to_across[h].start()
        to_beside[h].start()

    late = place >= (shards + 1) // 2

    @pl.when(late)
    def _():
        lax.fori_loop(0, chunks, one_chunk, 0)

    for h in range(heads):

        @pl.when(place == 0)
        def _():
            state_ref[h] = init_ref[h]

        @pl.when(place > 0)
        def _():
            chain(h).wait_recv()
            state_ref[h] = wire_in[h].astype(f32)

        @pl.when(place < shards - 1)
        def _():
            both = jnp.concatenate(split(state_ref[h]), axis=1)
            moved = dot(move_ref[h], jnp.concatenate([both, both], axis=0))
            moved = moved[:, :WIDTH] + moved[:, WIDTH:] + maps_ref[h, :, WIDTH:]
            wire_out[h] = moved.astype(wire_out.dtype)
            chain(h).start()

        @pl.when(late)
        def _():
            attend(h)

    @pl.when(jnp.logical_not(late))
    def _():
        lax.fori_loop(0, chunks, one_chunk, 0)
        for h in range(heads):
            attend(h)

    w_copy.wait()

    def project(slot, owner, first, count):
        rows = pl.multiple_of(owner * depth, depth) + first * WIDTH
        left = jnp.concatenate([att_ref[slot, first + i] for i in range(count)], axis=1)
        return dot(left, w_ref[pl.ds(pl.multiple_of(rows, WIDTH), count * WIDTH), :])

    acc_ref[...] = project(0, group, 0, heads)
    for h in range(heads):
        to_across[h].wait_recv()
        relayed[h].start()
        if h == 0:
            for i in range(heads):
                to_beside[i].wait_recv()
            acc_ref[...] += project(2, beside, 0, heads)
        if h % 2 == 1:
            acc_ref[...] += project(1, across, h - 1, 2)
            if h > 1:
                relayed[h - 3].wait_recv()
                relayed[h - 2].wait_recv()
                acc_ref[...] += project(3, beyond, h - 3, 2)
    relayed[heads - 2].wait_recv()
    relayed[heads - 1].wait_recv()
    out_ref[...] = (acc_ref[...] + project(3, beyond, heads - 2, 2)).astype(bf16)
    for h in range(heads):
        to_across[h].wait_send()
        to_beside[h].wait_send()
        relayed[h].wait_send()

        @pl.when(place < shards - 1)
        def _():
            chain(h).wait_send()


def layer(queries, key_pairs, value_pairs, init_state, out_weight, wire):
    heads = init_state.shape[0]
    shards = lax.axis_size("seq")
    tokens = queries.shape[0]
    chunks = tokens // CHUNK
    features = out_weight.shape[0]
    cols = out_weight.shape[1] // lax.axis_size("head")
    vmem = pl.BlockSpec(memory_space=pltpu.VMEM)
    dma = pltpu.SemaphoreType.DMA
    return pl.pallas_call(
        functools.partial(layer_kernel, shards, heads),
        in_specs=[vmem] * 4 + [pl.BlockSpec(memory_space=pl.ANY)],
        out_specs=vmem,
        out_shape=jax.ShapeDtypeStruct((tokens, cols), bf16),
        scratch_shapes=[
            pltpu.VMEM((heads, WIDTH, 2 * WIDTH), f32),
            pltpu.VMEM((chunks, heads, WIDTH, 2 * WIDTH), bf16),
            pltpu.VMEM((chunks, heads, MICRO, 2 * WIDTH), bf16),
            pltpu.VMEM((tokens, heads * WIDTH), bf16),
            pltpu.VMEM((tokens, heads * WIDTH), f32),
            pltpu.VMEM((features, cols), bf16),
            pltpu.VMEM((heads, WIDTH, 2 * WIDTH), bf16),
            pltpu.VMEM((heads, WIDTH, WIDTH), f32),
            pltpu.VMEM((heads, WIDTH, WIDTH), wire),
            pltpu.VMEM((heads, WIDTH, WIDTH), wire),
            pltpu.VMEM((4, heads, tokens, WIDTH), bf16),
            pltpu.VMEM((tokens, cols), f32),
            dma, dma((heads,)), dma((heads,)), dma((4, heads)), dma((4, heads)),
        ],
        compiler_params=pltpu.CompilerParams(
            vmem_limit_bytes=56 * 2**20, collective_id=0, has_side_effects=True
        ),
        name="layer",
    )(queries, key_pairs, value_pairs, init_state, out_weight)


def local(queries, key_pairs, value_pairs, init_state, out_weight):
    wire = bf16 if lax.axis_size("seq") <= 8 else f32
    return layer(queries, key_pairs, value_pairs, init_state, out_weight, wire)


def solution(mesh):
    in_specs = (
        P("seq", "head"),
        P("seq", None, "head"),
        P("seq", None, "head"),
        P("head", None, None),
        P(),
    )
    out_specs = P("seq", "head")
    return jax.shard_map(local, mesh=mesh, in_specs=in_specs, out_specs=out_specs, check_vma=False)
```

```python
import functools

import jax
import jax.numpy as jnp
from jax import lax
from jax.experimental import pallas as pl
from jax.experimental.pallas import tpu as pltpu
from jax.sharding import PartitionSpec as P

WIDTH = 128
CHUNK = 64
MICRO = 2 * CHUNK
SMALL = 8
epsilon = 1e-06
f32, bf16 = jnp.float32, jnp.bfloat16


def dot(a, b, dims=((1,), (0,))):
    return lax.dot_general(a, b, (dims, ((), ())), preferred_element_type=f32)


def split(x):
    high = x.astype(bf16)
    return high, (x - high.astype(f32)).astype(bf16)


def wide_left(x):
    return jnp.concatenate(split(x), axis=1)


def wide_right(y):
    row = jnp.concatenate(split(y), axis=1)
    return jnp.concatenate([row, row], axis=0)


def exact_product(x, y):
    both = dot(wide_left(x), wide_right(y))
    half = y.shape[1]
    return both[:, :half] + both[:, half:]


def iota(shape, dim):
    return lax.broadcasted_iota(jnp.int32, shape, dim)


def small_inverse(lower):
    row, col = iota((MICRO, WIDTH), 0), iota((MICRO, WIDTH), 1)
    same = row // SMALL == col // SMALL
    packed = jnp.where(same, lower, 0.0).reshape(MICRO // SMALL, SMALL, WIDTH).sum(0)
    sub, lane = iota((SMALL, WIDTH), 0), iota((SMALL, WIDTH), 1)
    inverse = jnp.where(lane % SMALL == sub, 1.0, 0.0).astype(f32)
    for c in range(SMALL - 1):
        factor = jnp.take_along_axis(packed, lane // SMALL * SMALL + c, axis=1, mode="promise_in_bounds")
        inverse = inverse - factor * inverse[c : c + 1]
    return jnp.where(same, jnp.concatenate([inverse] * (MICRO // SMALL), axis=0), 0.0)


def odd_rows(x, b):
    return jnp.concatenate([x[i : i + b] for i in range(b, MICRO, 2 * b)], axis=0)


def weave(even, odd, b):
    rows = []
    for i in range(0, MICRO // 2, b):
        rows += [even[i : i + b], odd[i : i + b]]
    return jnp.concatenate(rows, axis=0)


def even_rows(x, b):
    return jnp.concatenate([x[i : i + b] for i in range(0, MICRO, 2 * b)], axis=0)


def unit_lower_inverses(lowers):
    inverses = [small_inverse(lower) for lower in lowers]
    half = MICRO // 2
    row, col = iota((half, WIDTH), 0), iota((half, WIDTH), 1)
    zeros = jnp.zeros((half, WIDTH), f32)
    b = SMALL
    while b < MICRO:
        below = col // b == row // b * 2
        firsts = [
            exact_product(jnp.where(below, odd_rows(lower, b), 0.0), inverse)
            for lower, inverse in zip(lowers, inverses)
        ]
        odds = [odd_rows(inverse, b) for inverse in inverses]
        seconds = [
            odd - exact_product(odd, weave(zeros, first, b)) for odd, first in zip(odds, firsts)
        ]
        inverses = [
            weave(even_rows(inverse, b), second, b) for inverse, second in zip(inverses, seconds)
        ]
        b *= 2
    return inverses


def pair_rows(ref, p, h):
    pairs = ref[pl.ds(p * CHUNK, CHUNK), :, h * WIDTH : (h + 1) * WIDTH]
    return pairs.reshape(MICRO, WIDTH)


def advance(step, heads, per_step, k_ref, v_ref, z_ref, start_ref, write_ref):
    base = step * per_step
    row, col = iota((MICRO, WIDTH), 0), iota((MICRO, WIDTH), 1)
    eye = jnp.where(row == col, 1.0, 0.0).astype(f32)

    where = [(p, h) for p in range(per_step) for h in range(heads)]

    def key_of(p, h):
        return pair_rows(k_ref, base + p, h)

    lowers, scales = [], []
    for p, h in where:
        key = key_of(p, h)
        gram = dot(key, key, ((1,), (1,)))
        diagonal = jnp.where(row == col, gram, 0.0)
        down = lax.rsqrt(jnp.sum(diagonal, axis=1, keepdims=True) + epsilon)
        across = lax.rsqrt(jnp.sum(diagonal, axis=0, keepdims=True) + epsilon)
        lowers.append(jnp.where(row > col, 2.0 * gram * down * across, 0.0))
        scales.append((down, across))
    inverses = unit_lower_inverses(lowers)
    prepared = []
    for (p, h), inverse, (down, across) in zip(where, inverses, scales):
        key = key_of(p, h)
        value = pair_rows(v_ref, base + p, h)
        inverse = inverse * (2.0 * down)
        write_key = dot(wide_left(inverse * across), jnp.concatenate([key, key], axis=0))
        write_value = dot(wide_left(inverse), jnp.concatenate([value, value], axis=0))
        (wk_high, wk_low), (wv_high, wv_low) = split(write_key), split(write_value)
        effect = dot(
            key, jnp.concatenate([wk_high, wv_high, wk_low, wv_low], axis=1), ((0,), (0,))
        )
        effect = effect[:, : 2 * WIDTH] + effect[:, 2 * WIDTH :]
        move, carry = eye - effect[:, :WIDTH], effect[:, WIDTH:]
        write_ref[base + p, h] = jnp.concatenate([wk_high, wv_high], axis=1)
        prepared.append((wide_left(move), carry))
    for (p, h), (move, carry) in zip(where, prepared):
        high, low = split(z_ref[h])
        start_ref[base + p, h] = high
        both = jnp.concatenate([high, low], axis=1)
        moved = dot(move, jnp.concatenate([both, both], axis=0))
        moved = moved[:, : 2 * WIDTH] + moved[:, 2 * WIDTH :]
        z_ref[h] = jnp.concatenate([moved[:, :WIDTH], moved[:, WIDTH:] + carry], axis=1)


def prepare(chunk, heads, q_ref, k_ref, start_ref, write_ref, a_ref, o_ref):
    rows = pl.ds(pl.multiple_of(chunk * CHUNK, CHUNK), CHUNK)
    token, micro = iota((CHUNK, MICRO), 0), iota((CHUNK, MICRO), 1)
    for h in range(heads):
        cols = slice(h * WIDTH, (h + 1) * WIDTH)
        query = q_ref[rows, cols]
        scores = dot(query, pair_rows(k_ref, chunk, h), ((1,), (1,)))
        scores = jnp.where(micro <= 2 * token + 1, scores, 0.0).astype(bf16)
        inner = dot(scores, write_ref[chunk, h])
        query = query.astype(f32)
        size = lax.rsqrt(jnp.sum(query * query, axis=1, keepdims=True) + epsilon)
        adjusted = (query - inner[:, :WIDTH]) * size
        out = dot(adjusted.astype(bf16), start_ref[chunk, h])
        a_ref[rows, cols] = out[:, :WIDTH].astype(bf16)
        o_ref[rows, cols] = out[:, WIDTH:] + inner[:, WIDTH:] * size


def layer_kernel(
    shards, heads, q_ref, k_ref, v_ref, init_ref, w_hbm, out_ref,
    maps_ref, start_ref, write_ref, a_ref, o_ref, w_ref, move_ref, state_ref, wire_out, wire_in, att_ref, acc_ref,
    w_sem, chain_send, chain_recv, att_send, att_recv,
):
    place, group = lax.axis_index("seq"), lax.axis_index("head")
    across = lax.rem(group + 2, 4)
    beside = group + 1 - 2 * lax.rem(group, 2)
    beyond = lax.rem(beside + 2, 4)
    depth, cols = heads * WIDTH, out_ref.shape[1]
    w_copy = pltpu.make_async_copy(
        w_hbm.at[:, pl.ds(pl.multiple_of(group * cols, cols), cols)], w_ref, w_sem
    )
    w_copy.start()

    barrier = pltpu.get_barrier_semaphore()

    def greet(target):
        pl.semaphore_signal(barrier, inc=1, device_id=target, device_id_type=pl.DeviceIdType.MESH)

    greet((place, across))
    greet((place, beside))

    @pl.when(place > 0)
    def _():
        greet((place - 1, group))

    @pl.when(place < shards - 1)
    def _():
        greet((place + 1, group))

    chunks, per_step = q_ref.shape[0] // CHUNK, 4
    eye = jnp.where(iota((WIDTH, WIDTH), 0) == iota((WIDTH, WIDTH), 1), 1.0, 0.0).astype(f32)
    for h in range(heads):
        maps_ref[h] = jnp.concatenate([eye, jnp.zeros((WIDTH, WIDTH), f32)], axis=1)

    def one_step(step, _):
        advance(step, heads, per_step, k_ref, v_ref, maps_ref, start_ref, write_ref)
        return 0

    def one_chunk(chunk, _):
        prepare(chunk, heads, q_ref, k_ref, start_ref, write_ref, a_ref, o_ref)
        return 0

    lax.fori_loop(0, chunks // per_step, one_step, 0)
    for h in range(heads):
        move_ref[h] = wide_left(maps_ref[h, :, :WIDTH])

    ends = jnp.where(place == 0, 1, 0) + jnp.where(place == shards - 1, 1, 0)
    pl.semaphore_wait(barrier, 4 - ends)

    def chain(h):
        return pltpu.make_async_remote_copy(
            src_ref=wire_out.at[h], dst_ref=wire_in.at[h],
            send_sem=chain_send.at[h], recv_sem=chain_recv.at[h],
            device_id=(place + 1, group), device_id_type=pl.DeviceIdType.MESH,
        )

    def pass_on(source, slot, h, target):
        return pltpu.make_async_remote_copy(
            src_ref=att_ref.at[source, h], dst_ref=att_ref.at[slot, h],
            send_sem=att_send.at[slot, h], recv_sem=att_recv.at[slot, h],
            device_id=(place, target), device_id_type=pl.DeviceIdType.MESH,
        )

    to_across = [pass_on(0, 1, h, across) for h in range(heads)]
    to_beside = [pass_on(0, 2, h, beside) for h in range(heads)]
    relayed = [pass_on(1, 3, h, beside) for h in range(heads)]

    def attend(h):
        here = slice(h * WIDTH, (h + 1) * WIDTH)
        att_ref[0, h] = (
            dot(a_ref[:, here], state_ref[h].astype(bf16)) + o_ref[:, here]
        ).astype(bf16)
        to_across[h].start()
        to_beside[h].start()

    late = place >= (shards + 1) // 2

    @pl.when(late)
    def _():
        lax.fori_loop(0, chunks, one_chunk, 0)

    for h in range(heads):

        @pl.when(place == 0)
        def _():
            state_ref[h] = init_ref[h]

        @pl.when(place > 0)
        def _():
            chain(h).wait_recv()
            state_ref[h] = wire_in[h].astype(f32)

        @pl.when(place < shards - 1)
        def _():
            both = jnp.concatenate(split(state_ref[h]), axis=1)
            moved = dot(move_ref[h], jnp.concatenate([both, both], axis=0))
            moved = moved[:, :WIDTH] + moved[:, WIDTH:] + maps_ref[h, :, WIDTH:]
            wire_out[h] = moved.astype(wire_out.dtype)
            chain(h).start()

        @pl.when(late)
        def _():
            attend(h)

    @pl.when(jnp.logical_not(late))
    def _():
        lax.fori_loop(0, chunks, one_chunk, 0)
        for h in range(heads):
            attend(h)

    w_copy.wait()

    def project(slot, owner, first, count):
        rows = pl.multiple_of(owner * depth, depth) + first * WIDTH
        left = jnp.concatenate([att_ref[slot, first + i] for i in range(count)], axis=1)
        return dot(left, w_ref[pl.ds(pl.multiple_of(rows, WIDTH), count * WIDTH), :])

    acc_ref[...] = project(0, group, 0, heads)
    for h in range(heads):
        to_across[h].wait_recv()
        relayed[h].start()
        if h == 0:
            for i in range(heads):
                to_beside[i].wait_recv()
            acc_ref[...] += project(2, beside, 0, heads)
        if h % 2 == 1:
            acc_ref[...] += project(1, across, h - 1, 2)
            if h > 1:
                relayed[h - 3].wait_recv()
                relayed[h - 2].wait_recv()
                acc_ref[...] += project(3, beyond, h - 3, 2)
    relayed[heads - 2].wait_recv()
    relayed[heads - 1].wait_recv()
    out_ref[...] = (acc_ref[...] + project(3, beyond, heads - 2, 2)).astype(bf16)
    for h in range(heads):
        to_across[h].wait_send()
        to_beside[h].wait_send()
        relayed[h].wait_send()

        @pl.when(place < shards - 1)
        def _():
            chain(h).wait_send()


def layer(queries, key_pairs, value_pairs, init_state, out_weight, wire):
    heads = init_state.shape[0]
    shards = lax.axis_size("seq")
    tokens = queries.shape[0]
    chunks = tokens // CHUNK
    features = out_weight.shape[0]
    cols = out_weight.shape[1] // lax.axis_size("head")
    vmem = pl.BlockSpec(memory_space=pltpu.VMEM)
    dma = pltpu.SemaphoreType.DMA
    return pl.pallas_call(
        functools.partial(layer_kernel, shards, heads),
        in_specs=[vmem] * 4 + [pl.BlockSpec(memory_space=pl.ANY)],
        out_specs=vmem,
        out_shape=jax.ShapeDtypeStruct((tokens, cols), bf16),
        scratch_shapes=[
            pltpu.VMEM((heads, WIDTH, 2 * WIDTH), f32),
            pltpu.VMEM((chunks, heads, WIDTH, 2 * WIDTH), bf16),
            pltpu.VMEM((chunks, heads, MICRO, 2 * WIDTH), bf16),
            pltpu.VMEM((tokens, heads * WIDTH), bf16),
            pltpu.VMEM((tokens, heads * WIDTH), f32),
            pltpu.VMEM((features, cols), bf16),
            pltpu.VMEM((heads, WIDTH, 2 * WIDTH), bf16),
            pltpu.VMEM((heads, WIDTH, WIDTH), f32),
            pltpu.VMEM((heads, WIDTH, WIDTH), wire),
            pltpu.VMEM((heads, WIDTH, WIDTH), wire),
            pltpu.VMEM((4, heads, tokens, WIDTH), bf16),
            pltpu.VMEM((tokens, cols), f32),
            dma, dma((heads,)), dma((heads,)), dma((4, heads)), dma((4, heads)),
        ],
        compiler_params=pltpu.CompilerParams(
            vmem_limit_bytes=56 * 2**20, collective_id=0, has_side_effects=True
        ),
        name="layer",
    )(queries, key_pairs, value_pairs, init_state, out_weight)


def local(queries, key_pairs, value_pairs, init_state, out_weight):
    wire = bf16 if lax.axis_size("seq") <= 8 else f32
    return layer(queries, key_pairs, value_pairs, init_state, out_weight, wire)


def solution(mesh):
    in_specs = (
        P("seq", "head"),
        P("seq", None, "head"),
        P("seq", None, "head"),
        P("head", None, None),
        P(),
    )
    out_specs = P("seq", "head")
    return jax.shard_map(local, mesh=mesh, in_specs=in_specs, out_specs=out_specs, check_vma=False)
```
